32 devices in a mesh: grp: 2 (over x), tx: 8 (over z, y), ty: 2 (over core).
Axes of the slice: x: 2, y: 2, z: 4, core: 2. Of those that a mesh axis runs over, the one named last changes fastest.
Arguments:
- raster: bfloat16 [128, 16, 128, 128], P(('grp', 'tx'), 'ty'), parts along dimension 0, may hold values from 0 to 1
- kernels: bfloat16 [128, 4096], replicated, may hold values from -0.5 to 0.5
- kernel_weights: float32 [16], replicated, may hold values from 0.05 to 1
- cut_weights: float32 [128], replicated, may hold values from -0.3 to 0.3
- need_list: int32 [16, 2, 84], P(('grp', 'tx'), 'ty'), parts along dimension 0, may hold values from 0 to 99, as said below
- point_slot: int32 [16, 2, 3072], P(('grp', 'tx'), 'ty'), parts along dimension 0, may hold values from 0 to 83, as said below
- point_row: int32 [16, 2, 3072], P(('grp', 'tx'), 'ty'), parts along dimension 0, may hold values from 0 to 127
- threshold: float32 [16, 2, 3072], P(('grp', 'tx'), 'ty'), parts along dimension 0, may hold values from -2 to 2
- point_weight: float32 [16, 2, 3072], P(('grp', 'tx'), 'ty'), parts along dimension 0, may hold values from 1 to 48
- jac_ids: int32 [16, 2, 24, 4], P(('grp', 'tx'), 'ty'), parts along dimension 0, may hold values from 0 to 59
- jacobian: float32 [16, 2, 24, 4, 128, 128], P(('grp', 'tx'), 'ty'), parts along dimension 0, may hold values from -0.25 to 0.25
Outputs:
- epe: float32 [16, 2, 3072], P(('grp', 'tx'), 'ty'), parts along dimension 0
- step: float32 [16, 2, 1536], P(('grp', 'tx'), 'ty'), parts along dimension 0
The draws below stay inside these ranges and needn't reach their ends.
There are 2 independent parts, one for each index of `grp`. The reference program is written for one: setup_inputs(seed, part) draws one part's arguments, and reference() takes and returns one part's arrays. A program takes and returns all parts, laid end to end along the dimension named above; an argument that names none is the same for every part. Nothing has to cross between parts.
Inputs may be any that keep to these rules, and one draw needn't show every extreme that they name: `need_list`: each tile's list names 84 distinct blocks of its extended grid: all 64 blocks it owns and 20 of the cycle around them. `point_slot`: each need-list entry that names a cycle block is named by exactly 16 cut lines of the tile; all other cut lines name owned blocks.
All inputs are finite; a program needn't handle non-finite values.
Results may differ from the reference program's by a relative error of at most 0.0003.
Values may be sent and summed in bfloat16 or wider, within the bound.
A program may use at most 64 MiB of HBM per device.

```python
import math
import jax
import jax.numpy as jnp
import numpy as np
from jax import lax

BS = 128
NK = 16
GX = 8
GY = 8
CYCLE = 20
PB = 16
NEED = 84
P_SIZE = 3072
SEG = 1536
NNZ = 4
ITERS = 3
NXB = 64
NYB = 16
N_TX = 8
N_TY = 2


def border_flags():
    row_span = GY + 2
    return np.array([1 if a == 0 or b == 0 or a == GX + 1 or (b == GY + 1) else 0 for a in range(GX + 2) for b in range(row_span)], dtype=np.int32)


def listed_blocks(key):
    row_span = GY + 2
    interior = np.array([(a + 1) * row_span + b + 1 for a in range(GX) for b in range(GY)], dtype=np.int32)
    border = np.array([a * row_span + b for a in range(GX + 2) for b in range(row_span) if a == 0 or b == 0 or a == GX + 1 or (b == GY + 1)], dtype=np.int32)
    key_list = jax.random.split(key, N_TX * N_TY)

    def pick_tile(tile_key):
        key_one, key_two = jax.random.split(tile_key)
        chosen = jax.random.permutation(key_one, jnp.asarray(border))[:CYCLE]
        joined = jnp.concatenate([jnp.asarray(interior), chosen])
        return jax.random.permutation(key_two, joined)
    return jax.vmap(pick_tile)(key_list).reshape(N_TX, N_TY, NEED).astype(jnp.int32)


def draw_need_list(key, part):
    listed = listed_blocks(key)
    return listed


def draw_point_slot(key, part):
    listed = listed_blocks(key)
    key = jax.random.fold_in(key, 13)
    flags = jnp.asarray(border_flags())
    key_list = jax.random.split(key, N_TX * N_TY)

    def place(tile_key, tile_list):
        key_one, key_two = jax.random.split(tile_key)
        is_cycle = flags[tile_list]
        order = jnp.argsort(1 - is_cycle, stable=True).astype(jnp.int32)
        cycle_part = order[jnp.arange(CYCLE * PB, dtype=jnp.int32) // PB]
        inner_part = order[CYCLE + jax.random.randint(key_one, (P_SIZE - CYCLE * PB,), 0, GX * GY)]
        joined = jnp.concatenate([cycle_part, inner_part])
        return jax.random.permutation(key_two, joined)
    placed = jax.vmap(place)(key_list, listed.reshape(N_TX * N_TY, NEED))
    return placed.reshape(N_TX, N_TY, P_SIZE).astype(jnp.int32)


def draw_point_weight(key, part):
    key = jax.random.fold_in(key, 11)
    position = jnp.arange(N_TX, dtype=jnp.float32) / max(N_TX - 1, 1)
    levels = jnp.exp(position * math.log(3.0))
    spread = jnp.exp(jax.random.uniform(key, (N_TX, N_TY, P_SIZE), jnp.float32, 0.0, math.log(10.0)))
    return (levels[:, None, None] * spread).astype(jnp.float32)


def place_ends(values, own_key, smallest, top_value):
    longest = values.shape.index(max(values.shape))
    spots = []
    for shift in (0, 1):
        where = [jax.random.randint(jax.random.fold_in(own_key, axis), (), 0, length) for axis, length in enumerate(values.shape)]
        where[longest] = (where[longest] + shift) % values.shape[longest]
        spots.append(tuple(where))
    return values.at[spots[0]].set(smallest).at[spots[1]].set(top_value)


def block_levels(stream_key, shape, cuts, low, largest):
    factor_of, own = 1.0, jax.random.fold_in(stream_key, 6)
    for dim, shards_of in cuts:
        steps = jnp.exp(jax.random.uniform(jax.random.fold_in(own, dim), (shards_of,), jnp.float32, low / len(cuts), largest / len(cuts)))
        factor_of = factor_of * jnp.repeat(steps, shape[dim] // shards_of).reshape([-1 if axis == dim else 1 for axis in range(len(shape))])
    return factor_of


def bell_draw(stream_key, dims, deviation, reach, shards=(), kind=jnp.bfloat16):
    loudness = block_levels(stream_key, dims, shards, -0.22, 0.18) if shards else 1.0
    values = jax.random.normal(stream_key, dims, jnp.float32) * deviation * loudness
    return jnp.minimum(jnp.maximum(values, -reach), reach).astype(kind)


def setup_inputs(seed: int = 0, part: int = 0) -> dict:
    seeds = jax.random.split(jax.random.key(seed), 12)
    own_keys = jax.random.split(jax.random.fold_in(seeds[11], part), 12)
    return {
        "raster": jnp.clip(1.0 * jax.random.uniform(own_keys[0], (NXB, NYB, BS, BS), jnp.float32) ** block_levels(own_keys[0], (NXB, NYB, BS, BS), ((0, 8), (1, 2)), -0.2, 0.2), 0.0, 1.0).astype(jnp.bfloat16),
        "kernels": bell_draw(seeds[1], (BS, 2 * NK * BS), BS ** -0.5, 0.5),
        "kernel_weights": jnp.clip(jnp.exp(jax.random.uniform(seeds[2], (NK,), jnp.float32, math.log(0.05), math.log(1.0))), 0.05, 1.0),
        "cut_weights": bell_draw(seeds[3], (BS,), 0.05, 0.3, (), jnp.float32),
        "need_list": draw_need_list(jax.random.fold_in(jax.random.fold_in(seeds[11], part), 71), part),
        "point_slot": draw_point_slot(jax.random.fold_in(jax.random.fold_in(seeds[11], part), 71), part),
        "point_row": place_ends(jax.random.randint(own_keys[6], (N_TX, N_TY, P_SIZE), 0, BS), jax.random.fold_in(own_keys[6], 1), 0, BS - 1).astype(jnp.int32),
        "threshold": jnp.clip(jax.random.uniform(own_keys[7], (N_TX, N_TY, P_SIZE), jnp.float32, -2.0, 2.0) * block_levels(own_keys[7], (N_TX, N_TY, P_SIZE), ((0, 8), (1, 2)), -0.4, 0.0), -2.0, 2.0),
        "point_weight": draw_point_weight(jax.random.fold_in(jax.random.fold_in(seeds[11], part), 71), part),
        "jac_ids": place_ends(jax.random.randint(own_keys[9], (N_TX, N_TY, P_SIZE // BS, NNZ), 0, 5 * (SEG // BS)), jax.random.fold_in(own_keys[9], 1), 0, (5 * (SEG // BS)) - 1).astype(jnp.int32),
        "jacobian": bell_draw(own_keys[10], (N_TX, N_TY, P_SIZE // BS, NNZ, BS, BS), (NNZ * BS) ** -0.5, 0.25, ((0, 8), (1, 2)), jnp.float32),
    }


damping = 1.0


def reference(raster, kernels, kernel_weights, cut_weights, need_list, point_slot, point_row, threshold, point_weight, jac_ids, jacobian):
    n_tiles = N_TX * N_TY
    seg_blocks = SEG // BS
    pt_blocks = P_SIZE // BS
    padded = jnp.pad(raster, ((1, 1), (1, 1), (0, 0), (0, 0)))
    weight_pair = jnp.repeat(kernel_weights, 2)

    def one_tile(pieces):
        tile_index, need_ids, slots, row_ids, levels = pieces
        tile_x = (tile_index // N_TY).astype(jnp.int32)
        tile_y = (tile_index % N_TY).astype(jnp.int32)
        extended = lax.dynamic_slice(padded, (tile_x * GX, tile_y * GY, jnp.int32(0), jnp.int32(0)), (GX + 2, GY + 2, BS, BS))
        flat_rows = extended.reshape(-1, BS)
        row_data = flat_rows[(need_ids[slots] * BS + row_ids).astype(jnp.int32)]
        amplitude = jnp.dot(row_data, kernels, preferred_element_type=jnp.float32).reshape(P_SIZE, 2 * NK, BS)
        intensity = jnp.einsum('pkc,k->pc', amplitude * amplitude, weight_pair, precision=lax.Precision.HIGHEST)
        return jnp.dot(intensity, cut_weights, precision=lax.Precision.HIGHEST) - levels

    epe = lax.map(one_tile, (jnp.arange(n_tiles, dtype=jnp.int32), need_list.reshape(n_tiles, NEED), point_slot.reshape(n_tiles, P_SIZE), point_row.reshape(n_tiles, P_SIZE), threshold.reshape(n_tiles, P_SIZE))).reshape(N_TX, N_TY, P_SIZE)

    seg_ids = jac_ids.reshape(n_tiles, pt_blocks * NNZ)
    jac_blocks = jacobian.reshape(n_tiles, pt_blocks, NNZ, BS, BS)

    def forward(vector):
        padded_v = jnp.pad(vector, ((1, 1), (1, 1), (0, 0)))
        beside_all = jnp.stack([padded_v[1:-1, 1:-1], padded_v[:-2, 1:-1], padded_v[2:, 1:-1], padded_v[1:-1, :-2], padded_v[1:-1, 2:]], axis=2)
        beside_all = beside_all.reshape(n_tiles, 5 * seg_blocks, BS)
        gathered = jax.vmap(lambda e, i: e[i])(beside_all, seg_ids).reshape(n_tiles, pt_blocks, NNZ, BS)
        result = jnp.einsum('tnkij,tnkj->tni', jac_blocks, gathered, precision=lax.Precision.HIGHEST)
        return result.reshape(N_TX, N_TY, P_SIZE)

    def backward(values):
        contrib = jnp.einsum('tnkij,tni->tnkj', jac_blocks, values.reshape(n_tiles, pt_blocks, BS), precision=lax.Precision.HIGHEST)
        contrib = contrib.reshape(n_tiles, pt_blocks * NNZ, BS)
        scattered = jax.vmap(lambda c, i: jnp.zeros((5 * seg_blocks, BS), c.dtype).at[i].add(c))(contrib, seg_ids)
        scattered = scattered.reshape(N_TX, N_TY, 5, SEG)
        pad_x = ((1, 1), (0, 0), (0, 0))
        pad_y = ((0, 0), (1, 1), (0, 0))
        total = scattered[:, :, 0]
        total = total + jnp.pad(scattered[:, :, 2], pad_x)[:-2]
        total = total + jnp.pad(scattered[:, :, 1], pad_x)[2:]
        total = total + jnp.pad(scattered[:, :, 4], pad_y)[:, :-2]
        total = total + jnp.pad(scattered[:, :, 3], pad_y)[:, 2:]
        return total

    def apply_normal(vector):
        return backward(point_weight * forward(vector)) + damping * vector

    rhs = -backward(point_weight * epe)
    step = jnp.zeros_like(rhs)
    residual, direction = rhs, rhs
    norm_now = jnp.sum(residual * residual)
    for turn in range(ITERS):
        image = apply_normal(direction)
        alpha = norm_now / jnp.sum(direction * image)
        step = step + alpha * direction
        residual = residual - alpha * image
        norm_next = jnp.sum(residual * residual)
        direction = residual + (norm_next / norm_now) * direction
        norm_now = norm_next
    return epe, step
```

```python
import functools

import jax
import jax.numpy as jnp
from jax import lax
from jax.experimental import pallas as pl
from jax.experimental.pallas import tpu as pltpu
from jax.sharding import PartitionSpec as P

BS = 128
SEG = 1536
ROWS = 16
MESH = pl.DeviceIdType.MESH
SIDES = ((0, 0), (-1, 0), (1, 0), (0, -1), (0, 1))
OPPOSITE = (0, 2, 1, 4, 3)
ITERS = 3


def split_3(value):
    high = value.astype(jnp.bfloat16)
    rest = value - high.astype(jnp.float32)
    middle = rest.astype(jnp.bfloat16)
    low = (rest - middle.astype(jnp.float32)).astype(jnp.bfloat16)
    return high, middle, low


def split_2(value):
    high = value.astype(jnp.bfloat16)
    low = (value - high.astype(jnp.float32)).astype(jnp.bfloat16)
    return high, low


def select_3(chooser, value):
    parts = split_3(value)
    total = jnp.dot(chooser, parts[2], preferred_element_type=jnp.float32)
    total = total + jnp.dot(chooser, parts[1], preferred_element_type=jnp.float32)
    return total + jnp.dot(chooser, parts[0], preferred_element_type=jnp.float32)


def kernel(
    n_tx,
    n_ty,
    raster_hbm,
    kernels_hbm,
    kw_ref,
    cw_ref,
    need_ref,
    slot_ref,
    row_ref,
    level_ref,
    weight_ref,
    ids_ref,
    jac_hbm,
    epe_ref,
    step_ref,
    raster_v,
    kernels_v,
    jac_v,
    q_own,
    edge_x,
    edge_y,
    halo_x,
    halo_y,
    q_ext,
    need_pad,
    choose,
    vec,
    gathered,
    contrib,
    w_cols,
    u_cols,
    w_pad,
    sent,
    arrived,
    part_sums,
    all_sums,
    local_sem,
    hx_send,
    hx_recv,
    hy_send,
    hy_recv,
    ex_send,
    ex_recv,
    sum_send,
    sum_recv,
):
    n_dev = n_tx * n_ty
    gx, gy = raster_hbm.shape[0], raster_hbm.shape[1]
    pt_blocks = slot_ref.shape[1] // BS
    nnz = ids_ref.shape[1]
    seg_blocks = step_ref.shape[1] // BS
    n_kern = kw_ref.shape[0]
    span_y = gy + 2
    need = need_ref.shape[1]
    tx, ty = lax.axis_index("tx"), lax.axis_index("ty")
    rank = tx * n_ty + ty

    copy_k = pltpu.make_async_copy(kernels_hbm, kernels_v, local_sem.at[0])
    copy_r = pltpu.make_async_copy(raster_hbm, raster_v, local_sem.at[1])
    copy_j = pltpu.make_async_copy(jac_hbm, jac_v, local_sem.at[2])
    copy_k.start()
    copy_r.start()
    copy_j.start()

    def present(dx, dy):
        ok = None
        for pos, delta, count in ((tx, dx, n_tx), (ty, dy, n_ty)):
            test = None
            if delta < 0:
                test = pos + delta >= 0
            elif delta > 0:
                test = pos + delta < count
            if test is not None:
                ok = test if ok is None else jnp.logical_and(ok, test)
        return ok

    halo_x[...] = jnp.zeros_like(halo_x)
    halo_y[...] = jnp.zeros_like(halo_y)
    arrived[...] = jnp.zeros_like(arrived)

    barrier = pltpu.get_barrier_semaphore()

    def other(offset):
        peer = lax.rem(rank + offset, n_dev)
        return peer, {"tx": peer // n_ty, "ty": lax.rem(peer, n_ty)}

    @pl.loop(1, n_dev)
    def _(offset):
        pl.semaphore_signal(barrier, inc=1, device_id=other(offset)[1], device_id_type=MESH)

    copy_k.wait()
    cut = cw_ref[...]
    both = jnp.zeros((2 * BS, BS), jnp.float32)
    width = 4 * BS
    for chunk in range(2 * n_kern * BS // width):
        piece = kernels_v[:, chunk * width : (chunk + 1) * width]
        factor = jnp.concatenate(
            [cut * kw_ref[(chunk * 4 + i) // 2] for i in range(4)], axis=1
        )
        high, low = split_2(piece.astype(jnp.float32) * factor)
        both = both + lax.dot_general(
            jnp.concatenate([high, low], axis=0),
            piece,
            (((1,), (1,)), ((), ())),
            preferred_element_type=jnp.float32,
        )
    form = jnp.concatenate(split_2(both[:BS] + both[BS:]), axis=1)

    copy_r.wait()
    eye = lax.broadcasted_iota(jnp.int32, (1, BS, BS), 1) == lax.broadcasted_iota(
        jnp.int32, (1, BS, BS), 2
    )

    @pl.loop(0, gx)
    def _(a):
        rows = raster_v[a].reshape(gy * BS, BS)
        product = jnp.dot(rows, form, preferred_element_type=jnp.float32)
        terms = (product[:, :BS] + product[:, BS:]) * rows.astype(jnp.float32)
        column = jnp.sum(terms.reshape(gy, BS, BS), axis=2, keepdims=True)
        q = jnp.sum(jnp.where(eye, column, 0.0), axis=1)
        q_own[a] = q
        edge_y[0, pl.ds(a, 1), :] = q[0:1]
        edge_y[1, pl.ds(a, 1), :] = q[gy - 1 : gy]

    edge_x[0] = q_own[0]
    edge_x[1] = q_own[gx - 1]

    pl.semaphore_wait(barrier, n_dev - 1)

    halo_copies = []
    for side, dx in ((0, -1), (1, 1)):
        for dy in (-1, 0, 1):
            halo_copies.append(
                (
                    (dx, dy),
                    pltpu.make_async_remote_copy(
                        src_ref=edge_x.at[side],
                        dst_ref=halo_x.at[1 - side, 1 - dy],
                        send_sem=hx_send.at[side, 1 + dy],
                        recv_sem=hx_recv.at[1 - side, 1 - dy],
                        device_id={"tx": tx + dx, "ty": ty + dy},
                        device_id_type=MESH,
                    ),
                )
            )
    for side, dy in ((0, -1), (1, 1)):
        halo_copies.append(
            (
                (0, dy),
                pltpu.make_async_remote_copy(
                    src_ref=edge_y.at[side],
                    dst_ref=halo_y.at[1 - side],
                    send_sem=hy_send.at[side],
                    recv_sem=hy_recv.at[1 - side],
                    device_id={"tx": tx, "ty": ty + dy},
                    device_id_type=MESH,
                ),
            )
        )
    for (dx, dy), copy in halo_copies:

        @pl.when(present(dx, dy))
        def _():
            copy.start()

    q_ext[...] = jnp.zeros_like(q_ext)
    for a in range(gx):
        start = (a + 1) * span_y + 1
        q_ext[start : start + gy, :] = q_own[a]
    need_pad[...] = jnp.full(need_pad.shape, -1, jnp.int32)
    need_pad[:, :need] = need_ref[...]
    listed = (lax.broadcasted_iota(jnp.int32, (BS, BS), 0) == need_pad[...]).astype(jnp.float32).astype(
        jnp.bfloat16
    )
    choose[...] = jnp.zeros_like(choose)
    ids = ids_ref[...]
    for t in range(1, 5):
        ids = ids + jnp.where(ids_ref[...] >= t * seg_blocks, ROWS - seg_blocks, 0)
    for k in range(nnz):
        choose[k * pt_blocks : (k + 1) * pt_blocks, :] = (
            lax.broadcasted_iota(jnp.int32, (pt_blocks, BS), 1) == ids[:, k : k + 1]
        ).astype(jnp.float32)
    pick = choose[...].astype(jnp.bfloat16)
    pick_t = choose[...].T.astype(jnp.bfloat16)
    contrib[...] = jnp.zeros_like(contrib)
    vec[...] = jnp.zeros_like(vec)
    w_pad[...] = jnp.zeros_like(w_pad)
    for n in range(pt_blocks):
        w_pad[n : n + 1, :] = weight_ref[:, n * BS : (n + 1) * BS]
    turned = w_pad[...].T
    for n in range(pt_blocks):
        w_cols[n] = jnp.broadcast_to(turned[:, n : n + 1], (BS, BS))

    for side, dx in ((0, -1), (1, 1)):
        for dy in (-1, 0, 1):

            @pl.when(present(dx, dy))
            def _():
                pltpu.make_async_remote_copy(
                    src_ref=edge_x.at[side],
                    dst_ref=halo_x.at[side, 1 + dy],
                    send_sem=hx_send.at[side, 1 + dy],
                    recv_sem=hx_recv.at[side, 1 + dy],
                    device_id={"tx": tx + dx, "ty": ty + dy},
                    device_id_type=MESH,
                ).wait_recv()

    for side, dy in ((0, -1), (1, 1)):

        @pl.when(present(0, dy))
        def _():
            pltpu.make_async_remote_copy(
                src_ref=edge_y.at[side],
                dst_ref=halo_y.at[side],
                send_sem=hy_send.at[side],
                recv_sem=hy_recv.at[side],
                device_id={"tx": tx, "ty": ty + dy},
                device_id_type=MESH,
            ).wait_recv()

    for side in (0, 1):
        base = 0 if side == 0 else (gx + 1) * span_y
        q_ext[base + 1 : base + 1 + gy, :] = halo_x[side, 1]
        q_ext[base : base + 1, :] = halo_x[side, 0, gy - 1 : gy, :]
        q_ext[base + gy + 1 : base + gy + 2, :] = halo_x[side, 2, 0:1, :]
        for a in range(gx):
            at = (a + 1) * span_y + (0 if side == 0 else gy + 1)
            q_ext[at : at + 1, :] = halo_y[side, a : a + 1, :]

    table = jnp.concatenate(split_2(q_ext[...].T), axis=0)
    table = jnp.dot(table, listed, preferred_element_type=jnp.float32).astype(jnp.bfloat16)
    group = 2 * BS
    position = lax.broadcasted_iota(jnp.int32, (BS, group), 0)
    for piece in range(pt_blocks * BS // group):
        part = slice(piece * group, (piece + 1) * group)
        entry = (position == slot_ref[:, part]).astype(jnp.float32).astype(jnp.bfloat16)
        found = jnp.dot(table, entry, preferred_element_type=jnp.float32)
        found = found[:BS] + found[BS:]
        value = jnp.sum(
            jnp.where(position == row_ref[:, part], found, 0.0), axis=0, keepdims=True
        )
        error = value - level_ref[:, part]
        epe_ref[:, part] = error
        pulled = error * weight_ref[:, part]
        for i in range(group // BS):
            n = piece * (group // BS) + i
            w_pad[n : n + 1, :] = pulled[:, i * BS : (i + 1) * BS]
    turned = w_pad[...].T
    for n in range(pt_blocks):
        u_cols[n] = jnp.broadcast_to(turned[:, n : n + 1], (BS, BS))

    copy_j.wait()

    def part_copy(turn, t, t_here):
        return pltpu.make_async_remote_copy(
            src_ref=sent.at[turn, t],
            dst_ref=arrived.at[turn, t_here],
            send_sem=ex_send.at[turn, t],
            recv_sem=ex_recv.at[turn, t_here],
            device_id={"tx": tx + SIDES[t][0], "ty": ty + SIDES[t][1]},
            device_id_type=MESH,
        )

    def exchange(turn, parts):
        for t in range(1, 5):
            sent[turn, t] = parts[t]
        for t in range(1, 5):

            @pl.when(present(*SIDES[t]))
            def _():
                part_copy(turn, t, OPPOSITE[t]).start()

    def receive(turn):
        for t in range(1, 5):

            @pl.when(present(*SIDES[t]))
            def _():
                part_copy(turn, t, t).wait_recv()

        return [arrived[turn, t] for t in range(1, 5)]

    def finish(turn):
        summed = select_3(pick_t, contrib[...])
        parts = [summed[t * ROWS : (t + 1) * ROWS] for t in range(5)]
        exchange(turn, parts)
        others = receive(turn)
        return parts[0] + (others[0] + others[1]) + (others[2] + others[3])

    @pl.loop(0, pt_blocks)
    def _(n):
        for k in range(nnz):
            contrib[pl.ds(k * pt_blocks + n, 1), :] = jnp.sum(
                jac_v[n, k] * u_cols[n], axis=0, keepdims=True
            )

    def spread(own, others):
        vec[0:ROWS, :] = own
        for t in range(1, 5):
            vec[t * ROWS : (t + 1) * ROWS, :] = others[t - 1]

    def apply_normal(turn, own):
        gathered[...] = select_3(pick, vec[...])

        @pl.loop(0, pt_blocks)
        def _(n):
            total = jac_v[n, 0] * gathered[pl.ds(n, 1), :]
            for k in range(1, nnz):
                total = total + jac_v[n, k] * gathered[pl.ds(k * pt_blocks + n, 1), :]
            scaled = jnp.sum(total, axis=1, keepdims=True) * w_cols[n]
            for k in range(nnz):
                contrib[pl.ds(k * pt_blocks + n, 1), :] = jnp.sum(
                    jac_v[n, k] * scaled, axis=0, keepdims=True
                )

        return finish(turn) + own

    def sum_copy(turn, offset):
        peer, where = other(offset)
        return pltpu.make_async_remote_copy(
            src_ref=part_sums.at[turn],
            dst_ref=all_sums.at[turn, rank],
            send_sem=sum_send.at[turn, offset],
            recv_sem=sum_recv.at[turn, rank],
            device_id=where,
            device_id_type=MESH,
        )

    def start_sums(turn, residual, image):
        both = jnp.concatenate(
            [
                jnp.sum(residual * residual, axis=0, keepdims=True),
                jnp.sum(residual * image, axis=0, keepdims=True),
            ],
            axis=0,
        )
        part_sums[turn] = both
        all_sums[turn, rank] = both

        @pl.loop(1, n_dev)
        def _(offset):
            sum_copy(turn, offset).start()

    def end_sums(turn):
        @pl.loop(1, n_dev)
        def _(offset):
            peer, where = other(offset)
            pltpu.make_async_remote_copy(
                src_ref=part_sums.at[turn],
                dst_ref=all_sums.at[turn, peer],
                send_sem=sum_send.at[turn, offset],
                recv_sem=sum_recv.at[turn, peer],
                device_id=where,
                device_id_type=MESH,
            ).wait_recv()

        total = jnp.sum(jnp.sum(all_sums[turn], axis=0), axis=1, keepdims=True)
        return total[0:1], total[1:2]

    residual = -finish(0)
    exchange(1, [residual] * 5)
    spread(residual, receive(1))
    image = apply_normal(2, residual)
    start_sums(0, residual, image)
    exchange(3, [image] * 5)
    image_others = receive(3)
    spread(image, image_others)
    second = apply_normal(4, image)
    exchange(5, [second] * 5)

    norm_now, product = end_sums(0)
    alpha = norm_now / product
    direction, along, beyond = residual, image, second
    step = alpha * direction
    residual = residual - alpha * along
    image = image - alpha * beyond
    start_sums(1, residual, image)
    second_others = receive(5)
    spread(image, [w - alpha * z for w, z in zip(image_others, second_others)])
    second = apply_normal(6, image)

    norm_next, product = end_sums(1)
    ratio = norm_next / norm_now
    alpha = norm_next / (product - ratio * norm_next / alpha)
    norm_now = norm_next
    direction = residual + ratio * direction
    along = image + ratio * along
    beyond = second + ratio * beyond
    step = step + alpha * direction
    residual = residual - alpha * along
    image = image - alpha * beyond
    start_sums(2, residual, image)

    for (dx, dy), copy in halo_copies:

        @pl.when(present(dx, dy))
        def _():
            copy.wait_send()

    for turn in range(7):
        for t in range(1, 5):

            @pl.when(present(*SIDES[t]))
            def _():
                part_copy(turn, t, OPPOSITE[t]).wait_send()

    for turn in range(3):

        @pl.loop(1, n_dev)
        def _(offset):
            sum_copy(turn, offset).wait_send()

    norm_next, product = end_sums(2)
    ratio = norm_next / norm_now
    alpha = norm_next / (product - ratio * norm_next / alpha)
    direction = residual + ratio * direction
    step = step + alpha * direction
    for j in range(seg_blocks):
        step_ref[:, j * BS : (j + 1) * BS] = step[j : j + 1, :]


def on_device(
    n_tx,
    n_ty,
    raster,
    kernels,
    kernel_weights,
    cut_weights,
    need_list,
    point_slot,
    point_row,
    threshold,
    point_weight,
    jac_ids,
    jacobian,
):
    points = point_slot.shape[-1]
    pt_blocks, nnz = jac_ids.shape[-2:]
    gx, gy = raster.shape[:2]
    segments = SEG
    n_dev = n_tx * n_ty
    f32 = jnp.float32
    vmem = pl.BlockSpec(memory_space=pltpu.VMEM)
    anywhere = pl.BlockSpec(memory_space=pl.ANY)
    smem = pl.BlockSpec(memory_space=pltpu.SMEM)
    dma = pltpu.SemaphoreType.DMA
    epe, step = pl.pallas_call(
        functools.partial(kernel, n_tx, n_ty),
        out_shape=(
            jax.ShapeDtypeStruct((1, points), f32),
            jax.ShapeDtypeStruct((1, segments), f32),
        ),
        in_specs=[anywhere, anywhere, smem] + [vmem] * 7 + [anywhere],
        out_specs=(vmem, vmem),
        scratch_shapes=[
            pltpu.VMEM(raster.shape, jnp.bfloat16),
            pltpu.VMEM(kernels.shape, jnp.bfloat16),
            pltpu.VMEM((pt_blocks, nnz, BS, BS), f32),
            pltpu.VMEM((gx, gy, BS), f32),
            pltpu.VMEM((2, gy, BS), f32),
            pltpu.VMEM((2, gx, BS), f32),
            pltpu.VMEM((2, 3, gy, BS), f32),
            pltpu.VMEM((2, gx, BS), f32),
            pltpu.VMEM((BS, BS), f32),
            pltpu.VMEM((1, BS), jnp.int32),
            pltpu.VMEM((BS, BS), f32),
            pltpu.VMEM((BS, BS), f32),
            pltpu.VMEM((BS, BS), f32),
            pltpu.VMEM((BS, BS), f32),
            pltpu.VMEM((pt_blocks, BS, BS), f32),
            pltpu.VMEM((pt_blocks, BS, BS), f32),
            pltpu.VMEM((BS, BS), f32),
            pltpu.VMEM((7, 5, ROWS, BS), f32),
            pltpu.VMEM((7, 5, ROWS, BS), f32),
            pltpu.VMEM((3, 2, BS), f32),
            pltpu.VMEM((3, n_dev, 2, BS), f32),
            dma((3,)),
            dma((2, 3)),
            dma((2, 3)),
            dma((2,)),
            dma((2,)),
            dma((7, 5)),
            dma((7, 5)),
            dma((3, n_dev)),
            dma((3, n_dev)),
        ],
        compiler_params=pltpu.CompilerParams(
            collective_id=0, has_side_effects=True, vmem_limit_bytes=48 * 1024 * 1024
        ),
    )(
        raster,
        kernels,
        kernel_weights,
        cut_weights.reshape(1, BS),
        need_list.reshape(1, -1),
        point_slot.reshape(1, points),
        point_row.reshape(1, points),
        threshold.reshape(1, points),
        point_weight.reshape(1, points),
        jac_ids.reshape(pt_blocks, nnz),
        jacobian.reshape(pt_blocks, nnz, BS, BS),
    )
    return epe.reshape(1, 1, points), step.reshape(1, 1, segments)


def solution(mesh):
    tiles = ("grp", "tx")
    in_specs = (
        P(tiles, "ty", None, None),
        P(),
        P(),
        P(),
        P(tiles, "ty", None),
        P(tiles, "ty", None),
        P(tiles, "ty", None),
        P(tiles, "ty", None),
        P(tiles, "ty", None),
        P(tiles, "ty", None, None),
        P(tiles, "ty", None, None, None, None),
    )
    out_specs = (P(tiles, "ty", None), P(tiles, "ty", None))
    return jax.shard_map(
        functools.partial(on_device, mesh.shape["tx"], mesh.shape["ty"]),
        mesh=mesh,
        in_specs=in_specs,
        out_specs=out_specs,
        check_vma=False,
    )
```

```python
import functools

import jax
import jax.numpy as jnp
from jax import lax
from jax.experimental import pallas as pl
from jax.experimental.pallas import tpu as pltpu
from jax.sharding import PartitionSpec as P

BS = 128
SEG = 1536
MESH = pl.DeviceIdType.MESH
SIDES = ((0, 0), (-1, 0), (1, 0), (0, -1), (0, 1))
SUMS = 3
TURNS = 2 + 1
UNROLL = 6
DAMPING = 1.0


def split_3(value):
    high = value.astype(jnp.bfloat16)
    rest = value - high.astype(jnp.float32)
    middle = rest.astype(jnp.bfloat16)
    low = (rest - middle.astype(jnp.float32)).astype(jnp.bfloat16)
    return high, middle, low


def split_2(value):
    high = value.astype(jnp.bfloat16)
    low = (value - high.astype(jnp.float32)).astype(jnp.bfloat16)
    return high, low


def routes(n_tx, n_ty):
    found = {}
    for t, (ax, ay) in enumerate(SIDES):
        for u, (bx, by) in enumerate(SIDES):
            offset = (ax - bx, ay - by)
            if offset != (0, 0) and abs(offset[0]) < n_tx and abs(offset[1]) < n_ty:
                found.setdefault(offset, []).append((t, u))
    return sorted(found.items())


def kernel(
    n_tx,
    n_ty,
    raster_hbm,
    kernels_hbm,
    kw_hbm,
    cw_hbm,
    need_hbm,
    slot_hbm,
    row_hbm,
    level_hbm,
    weight_hbm,
    ids_hbm,
    jac_hbm,
    epe_ref,
    step_ref,
    raster_v,
    kernels_v,
    jac_v,
    kw_ref,
    cw_ref,
    need_ref,
    slot_ref,
    row_ref,
    level_ref,
    weight_ref,
    ids_ref,
    ids_s,
    q_own,
    edge_x,
    edge_y,
    halo_x,
    halo_y,
    q_ext,
    need_pad,
    choose,
    vec,
    contrib,
    energy,
    w_cols,
    u_cols,
    w_pad,
    sent,
    arrived,
    part_sums,
    all_sums,
    local_sem,
    hx_send,
    hx_recv,
    hy_send,
    hy_recv,
    ex_send,
    ex_recv,
    sum_send,
    sum_recv,
):
    n_dev = n_tx * n_ty
    gx, gy = raster_hbm.shape[0], raster_hbm.shape[1]
    pt_blocks = ids_ref.shape[0]
    nnz = ids_ref.shape[1]
    seg_blocks = step_ref.shape[1] // BS
    n_kern = kw_ref.shape[0]
    span_y = gy + 2
    need = need_ref.shape[1]
    tx, ty = lax.axis_index("tx"), lax.axis_index("ty")
    rank = tx * n_ty + ty

    copy_k = pltpu.make_async_copy(kernels_hbm, kernels_v, local_sem.at[0])
    copy_r = pltpu.make_async_copy(raster_hbm, raster_v, local_sem.at[1])
    copy_j = pltpu.make_async_copy(jac_hbm, jac_v, local_sem.at[2])
    small = [
        pltpu.make_async_copy(source, target, local_sem.at[3 + i])
        for i, (source, target) in enumerate(
            (
                (kw_hbm, kw_ref),
                (cw_hbm, cw_ref),
                (need_hbm, need_ref),
                (slot_hbm, slot_ref),
                (row_hbm, row_ref),
                (level_hbm, level_ref),
                (weight_hbm, weight_ref),
                (ids_hbm, ids_ref),
                (ids_hbm, ids_s),
            )
        )
    ]
    small[0].start()
    small[1].start()
    copy_k.start()
    copy_r.start()
    for copy in small[2:]:
        copy.start()
    copy_j.start()

    def present(dx, dy):
        ok = None
        for pos, delta, count in ((tx, dx, n_tx), (ty, dy, n_ty)):
            test = None
            if delta < 0:
                test = pos + delta >= 0
            elif delta > 0:
                test = pos + delta < count
            if test is not None:
                ok = test if ok is None else jnp.logical_and(ok, test)
        return ok

    halo_x[...] = jnp.zeros_like(halo_x)
    halo_y[...] = jnp.zeros_like(halo_y)
    arrived[...] = jnp.zeros_like(arrived)
    ways = routes(n_tx, n_ty)

    barrier = pltpu.get_barrier_semaphore()

    def other(offset):
        peer = lax.rem(rank + offset, n_dev)
        return peer, {"tx": peer // n_ty, "ty": lax.rem(peer, n_ty)}

    @pl.loop(1, n_dev)
    def _(offset):
        pl.semaphore_signal(barrier, inc=1, device_id=other(offset)[1], device_id_type=MESH)

    small[0].wait()
    small[1].wait()
    copy_k.wait()
    cut = cw_ref[...]
    both = jnp.zeros((2 * BS, BS), jnp.float32)
    width = 4 * BS
    for chunk in range(2 * n_kern * BS // width):
        piece = kernels_v[:, chunk * width : (chunk + 1) * width]
        factor = jnp.concatenate(
            [cut * kw_ref[(chunk * 4 + i) // 2] for i in range(4)], axis=1
        )
        high, low = split_2(piece.astype(jnp.float32) * factor)
        both = both + lax.dot_general(
            jnp.concatenate([high, low], axis=0),
            piece,
            (((1,), (1,)), ((), ())),
            preferred_element_type=jnp.float32,
        )
    form = jnp.concatenate(split_2(both[:BS] + both[BS:]), axis=1)

    copy_r.wait()
    eye = lax.broadcasted_iota(jnp.int32, (1, BS, BS), 1) == lax.broadcasted_iota(
        jnp.int32, (1, BS, BS), 2
    )

    @pl.loop(0, gx)
    def _(a):
        rows = raster_v[a].reshape(gy * BS, BS)
        product = jnp.dot(rows, form, preferred_element_type=jnp.float32)
        terms = (product[:, :BS] + product[:, BS:]) * rows.astype(jnp.float32)
        column = jnp.sum(terms.reshape(gy, BS, BS), axis=2, keepdims=True)
        q = jnp.sum(jnp.where(eye, column, 0.0), axis=1)
        q_own[a] = q
        edge_y[0, pl.ds(a, 1), :] = q[0:1]
        edge_y[1, pl.ds(a, 1), :] = q[gy - 1 : gy]

    edge_x[0] = q_own[0]
    edge_x[1] = q_own[gx - 1]

    pl.semaphore_wait(barrier, n_dev - 1)

    halo_copies = []
    for side, dx in ((0, -1), (1, 1)):
        for dy in (-1, 0, 1):
            halo_copies.append(
                (
                    (dx, dy),
                    pltpu.make_async_remote_copy(
                        src_ref=edge_x.at[side],
                        dst_ref=halo_x.at[1 - side, 1 - dy],
                        send_sem=hx_send.at[side, 1 + dy],
                        recv_sem=hx_recv.at[1 - side, 1 - dy],
                        device_id={"tx": tx + dx, "ty": ty + dy},
                        device_id_type=MESH,
                    ),
                )
            )
    for side, dy in ((0, -1), (1, 1)):
        halo_copies.append(
            (
                (0, dy),
                pltpu.make_async_remote_copy(
                    src_ref=edge_y.at[side],
                    dst_ref=halo_y.at[1 - side],
                    send_sem=hy_send.at[side],
                    recv_sem=hy_recv.at[1 - side],
                    device_id={"tx": tx, "ty": ty + dy},
                    device_id_type=MESH,
                ),
            )
        )
    for (dx, dy), copy in halo_copies:

        @pl.when(present(dx, dy))
        def _():
            copy.start()

    q_ext[...] = jnp.zeros_like(q_ext)
    for a in range(gx):
        start = (a + 1) * span_y + 1
        q_ext[start : start + gy, :] = q_own[a]
    for copy in small[2:]:
        copy.wait()
    need_pad[...] = jnp.full(need_pad.shape, -1, jnp.int32)
    need_pad[:, :need] = need_ref[...]
    listed = (lax.broadcasted_iota(jnp.int32, (BS, BS), 0) == need_pad[...]).astype(jnp.float32).astype(
        jnp.bfloat16
    )
    choose[...] = jnp.zeros_like(choose)
    ids = ids_ref[...]
    for k in range(nnz):
        choose[k * pt_blocks : (k + 1) * pt_blocks, :] = (
            lax.broadcasted_iota(jnp.int32, (pt_blocks, BS), 1) == ids[:, k : k + 1]
        ).astype(jnp.float32)
    pick_t = choose[...].T[: vec.shape[0]].astype(jnp.bfloat16)
    pick_t = jnp.concatenate([pick_t] * 3, axis=1)
    contrib[...] = jnp.zeros_like(contrib)
    vec[...] = jnp.zeros_like(vec)
    w_pad[...] = jnp.zeros_like(w_pad)
    for n in range(pt_blocks):
        w_pad[n : n + 1, :] = weight_ref[:, n * BS : (n + 1) * BS]
    turned = w_pad[...].T
    for n in range(pt_blocks):
        w_cols[n] = jnp.broadcast_to(turned[:, n : n + 1], (BS, BS))

    for side, dx in ((0, -1), (1, 1)):
        for dy in (-1, 0, 1):

            @pl.when(present(dx, dy))
            def _():
                pltpu.make_async_remote_copy(
                    src_ref=edge_x.at[side],
                    dst_ref=halo_x.at[side, 1 + dy],
                    send_sem=hx_send.at[side, 1 + dy],
                    recv_sem=hx_recv.at[side, 1 + dy],
                    device_id={"tx": tx + dx, "ty": ty + dy},
                    device_id_type=MESH,
                ).wait_recv()

    for side, dy in ((0, -1), (1, 1)):

        @pl.when(present(0, dy))
        def _():
            pltpu.make_async_remote_copy(
                src_ref=edge_y.at[side],
                dst_ref=halo_y.at[side],
                send_sem=hy_send.at[side],
                recv_sem=hy_recv.at[side],
                device_id={"tx": tx, "ty": ty + dy},
                device_id_type=MESH,
            ).wait_recv()

    for side in (0, 1):
        base = 0 if side == 0 else (gx + 1) * span_y
        q_ext[base + 1 : base + 1 + gy, :] = halo_x[side, 1]
        q_ext[base : base + 1, :] = halo_x[side, 0, gy - 1 : gy, :]
        q_ext[base + gy + 1 : base + gy + 2, :] = halo_x[side, 2, 0:1, :]
        for a in range(gx):
            at = (a + 1) * span_y + (0 if side == 0 else gy + 1)
            q_ext[at : at + 1, :] = halo_y[side, a : a + 1, :]

    table = jnp.concatenate(split_2(q_ext[...].T), axis=0)
    table = jnp.dot(table, listed, preferred_element_type=jnp.float32).astype(jnp.bfloat16)
    group = 2 * BS
    position = lax.broadcasted_iota(jnp.int32, (BS, group), 0)
    for piece in range(pt_blocks * BS // group):
        part = slice(piece * group, (piece + 1) * group)
        entry = (position == slot_ref[:, part]).astype(jnp.float32).astype(jnp.bfloat16)
        found = jnp.dot(table, entry, preferred_element_type=jnp.float32)
        found = found[:BS] + found[BS:]
        value = jnp.sum(
            jnp.where(position == row_ref[:, part], found, 0.0), axis=0, keepdims=True
        )
        error = value - level_ref[:, part]
        epe_ref[:, part] = error
        pulled = error * weight_ref[:, part]
        for i in range(group // BS):
            n = piece * (group // BS) + i
            w_pad[n : n + 1, :] = pulled[:, i * BS : (i + 1) * BS]
    turned = w_pad[...].T
    for n in range(pt_blocks):
        u_cols[n] = jnp.broadcast_to(turned[:, n : n + 1], (BS, BS))

    copy_j.wait()

    def way_copy(turn, way, flip):
        dx, dy = ways[way][0]
        sign = -1 if flip else 1
        return pltpu.make_async_remote_copy(
            src_ref=sent.at[turn, way],
            dst_ref=arrived.at[turn, way],
            send_sem=ex_send.at[turn, way],
            recv_sem=ex_recv.at[turn, way],
            device_id={"tx": tx + sign * dx, "ty": ty + sign * dy},
            device_id_type=MESH,
        )

    def start_terms(turn):
        summed = jnp.dot(
            pick_t,
            jnp.concatenate(split_3(contrib[...]), axis=0),
            preferred_element_type=jnp.float32,
        )
        parts = [summed[t * seg_blocks : (t + 1) * seg_blocks] for t in range(5)]
        for way, (offset, pairs) in enumerate(ways):
            for i, (t, u) in enumerate(pairs):
                sent[turn, way, i * seg_blocks : (i + 1) * seg_blocks, :] = parts[t]

            @pl.when(present(*offset))
            def _():
                way_copy(turn, way, False).start()

        return parts

    def end_terms(turn, parts):
        for way, ((dx, dy), pairs) in enumerate(ways):

            @pl.when(present(-dx, -dy))
            def _():
                way_copy(turn, way, True).wait_recv()

        total = list(parts)
        for way, (offset, pairs) in enumerate(ways):
            for i, (t, u) in enumerate(pairs):
                total[u] = total[u] + arrived[turn, way, i * seg_blocks : (i + 1) * seg_blocks, :]
        for u in range(1, 5):
            total[u] = jnp.where(present(*SIDES[u]), total[u], 0.0)
        return total

    def segments(u):
        return slice(u * seg_blocks, (u + 1) * seg_blocks)

    def products(values, backward):
        for u in range(5):
            vec[segments(u), :] = values[u]
        energy[...] = jnp.zeros_like(energy)

        @pl.loop(0, pt_blocks, unroll=UNROLL)
        def _(n):
            total = jac_v[n, 0] * vec[pl.ds(ids_s[n, 0], 1), :]
            for k in range(1, nnz):
                total = total + jac_v[n, k] * vec[pl.ds(ids_s[n, k], 1), :]
            error = jnp.sum(total, axis=1, keepdims=True)
            scaled = error * w_cols[n]
            energy[...] += jnp.sum((scaled * error).reshape(BS // 8, 8, BS), axis=0)
            if backward:
                for k in range(nnz):
                    contrib[pl.ds(k * pt_blocks + n, 1), :] = jnp.sum(
                        jac_v[n, k] * scaled, axis=0, keepdims=True
                    )

    def sum_copy(turn, offset, slot):
        peer, where = other(offset)
        at = rank if slot is None else peer
        return pltpu.make_async_remote_copy(
            src_ref=part_sums.at[turn],
            dst_ref=all_sums.at[turn, at],
            send_sem=sum_send.at[turn, offset],
            recv_sem=sum_recv.at[turn, at],
            device_id=where,
            device_id_type=MESH,
        )

    def start_sums(turn, own):
        square = jnp.sum(own * own, axis=0, keepdims=True)
        cross = jnp.sum(energy[...], axis=0, keepdims=True) * (1.0 / BS) + DAMPING * square
        both = jnp.concatenate([square, cross], axis=0)
        part_sums[turn] = both
        all_sums[turn, rank] = both

        @pl.loop(1, n_dev, unroll=3)
        def _(offset):
            sum_copy(turn, offset, None).start()

    def end_sums(turn):
        @pl.loop(1, n_dev, unroll=3)
        def _(offset):
            sum_copy(turn, offset, "theirs").wait_recv()

        total = jnp.sum(jnp.sum(all_sums[turn], axis=0), axis=1, keepdims=True)
        return total[0:1], total[1:2]

    @pl.loop(0, pt_blocks, unroll=UNROLL)
    def _(n):
        for k in range(nnz):
            contrib[pl.ds(k * pt_blocks + n, 1), :] = jnp.sum(
                jac_v[n, k] * u_cols[n], axis=0, keepdims=True
            )

    residual = [-part for part in end_terms(0, start_terms(0))]
    direction = along = step = norm_now = alpha = None
    for turn in range(SUMS):
        last = turn + 1 == SUMS
        products(residual, not last)
        if not last:
            parts = start_terms(turn + 1)
        start_sums(turn, residual[0])
        if last:
            for (dx, dy), copy in halo_copies:

                @pl.when(present(dx, dy))
                def _():
                    copy.wait_send()

            for before in range(TURNS):
                for way, (offset, pairs) in enumerate(ways):

                    @pl.when(present(*offset))
                    def _():
                        way_copy(before, way, False).wait_send()

            for before in range(SUMS):

                @pl.loop(1, n_dev, unroll=3)
                def _(offset):
                    sum_copy(before, offset, None).wait_send()

        else:
            image = [
                part + DAMPING * value
                for part, value in zip(end_terms(turn + 1, parts), residual)
            ]
        norm_next, product = end_sums(turn)
        if turn == 0:
            alpha = norm_next / product
            direction, step = residual[0], alpha * residual[0]
            along = image
        else:
            ratio = norm_next / norm_now
            alpha = norm_next / (product - ratio * norm_next / alpha)
            direction = residual[0] + ratio * direction
            step = step + alpha * direction
            if not last:
                along = [new + ratio * old for new, old in zip(image, along)]
        norm_now = norm_next
        if not last:
            residual = [value - alpha * change for value, change in zip(residual, along)]

    for j in range(seg_blocks):
        step_ref[:, j * BS : (j + 1) * BS] = step[j : j + 1, :]


def on_device(
    n_tx,
    n_ty,
    raster,
    kernels,
    kernel_weights,
    cut_weights,
    need_list,
    point_slot,
    point_row,
    threshold,
    point_weight,
    jac_ids,
    jacobian,
):
    points = point_slot.shape[-1]
    pt_blocks, nnz = jac_ids.shape[-2:]
    gx, gy = raster.shape[:2]
    segments = SEG
    wide = 2 * (SEG // BS)
    n_ways = len(routes(n_tx, n_ty))
    n_dev = n_tx * n_ty
    f32 = jnp.float32
    vmem = pl.BlockSpec(memory_space=pltpu.VMEM)
    anywhere = pl.BlockSpec(memory_space=pl.ANY)
    dma = pltpu.SemaphoreType.DMA
    epe, step = pl.pallas_call(
        functools.partial(kernel, n_tx, n_ty),
        out_shape=(
            jax.ShapeDtypeStruct((1, points), f32),
            jax.ShapeDtypeStruct((1, segments), f32),
        ),
        in_specs=[anywhere] * 11,
        out_specs=(vmem, vmem),
        scratch_shapes=[
            pltpu.VMEM(raster.shape, jnp.bfloat16),
            pltpu.VMEM(kernels.shape, jnp.bfloat16),
            pltpu.VMEM((pt_blocks, nnz, BS, BS), f32),
            pltpu.SMEM(kernel_weights.shape, f32),
            pltpu.VMEM((1, BS), f32),
            pltpu.VMEM((1, need_list.shape[-1]), jnp.int32),
            pltpu.VMEM((1, points), jnp.int32),
            pltpu.VMEM((1, points), jnp.int32),
            pltpu.VMEM((1, points), f32),
            pltpu.VMEM((1, points), f32),
            pltpu.VMEM((pt_blocks, nnz), jnp.int32),
            pltpu.SMEM((pt_blocks, nnz), jnp.int32),
            pltpu.VMEM((gx, gy, BS), f32),
            pltpu.VMEM((2, gy, BS), f32),
            pltpu.VMEM((2, gx, BS), f32),
            pltpu.VMEM((2, 3, gy, BS), f32),
            pltpu.VMEM((2, gx, BS), f32),
            pltpu.VMEM((BS, BS), f32),
            pltpu.VMEM((1, BS), jnp.int32),
            pltpu.VMEM((BS, BS), f32),
            pltpu.VMEM((64, BS), f32),
            pltpu.VMEM((BS, BS), f32),
            pltpu.VMEM((8, BS), f32),
            pltpu.VMEM((pt_blocks, BS, BS), f32),
            pltpu.VMEM((pt_blocks, BS, BS), f32),
            pltpu.VMEM((BS, BS), f32),
            pltpu.VMEM((TURNS, n_ways, wide, BS), f32),
            pltpu.VMEM((TURNS, n_ways, wide, BS), f32),
            pltpu.VMEM((SUMS, 2, BS), f32),
            pltpu.VMEM((SUMS, n_dev, 2, BS), f32),
            dma((12,)),
            dma((2, 3)),
            dma((2, 3)),
            dma((2,)),
            dma((2,)),
            dma((TURNS, n_ways)),
            dma((TURNS, n_ways)),
            dma((SUMS, n_dev)),
            dma((SUMS, n_dev)),
        ],
        compiler_params=pltpu.CompilerParams(
            collective_id=0, has_side_effects=True, vmem_limit_bytes=56 * 1024 * 1024
        ),
    )(
        raster,
        kernels,
        kernel_weights,
        cut_weights.reshape(1, BS),
        need_list.reshape(1, -1),
        point_slot.reshape(1, points),
        point_row.reshape(1, points),
        threshold.reshape(1, points),
        point_weight.reshape(1, points),
        jac_ids.reshape(pt_blocks, nnz),
        jacobian.reshape(pt_blocks, nnz, BS, BS),
    )
    return epe.reshape(1, 1, points), step.reshape(1, 1, segments)


def solution(mesh):
    tiles = ("grp", "tx")
    in_specs = (
        P(tiles, "ty", None, None),
        P(),
        P(),
        P(),
        P(tiles, "ty", None),
        P(tiles, "ty", None),
        P(tiles, "ty", None),
        P(tiles, "ty", None),
        P(tiles, "ty", None),
        P(tiles, "ty", None, None),
        P(tiles, "ty", None, None, None, None),
    )
    out_specs = (P(tiles, "ty", None), P(tiles, "ty", None))
    return jax.shard_map(
        functools.partial(on_device, mesh.shape["tx"], mesh.shape["ty"]),
        mesh=mesh,
        in_specs=in_specs,
        out_specs=out_specs,
        check_vma=False,
    )
```

```python
import functools

import jax
import jax.numpy as jnp
from jax import lax
from jax.experimental import pallas as pl
from jax.experimental.pallas import tpu as pltpu
from jax.sharding import PartitionSpec as P

BS = 128
SEG = 1536
MESH = pl.DeviceIdType.MESH
SIDES = ((0, 0), (-1, 0), (1, 0), (0, -1), (0, 1))
SUMS = 3
TURNS = 2 + 1
UNROLL = 6
DAMPING = 1.0


def split_3(value):
    high = value.astype(jnp.bfloat16)
    rest = value - high.astype(jnp.float32)
    middle = rest.astype(jnp.bfloat16)
    low = (rest - middle.astype(jnp.float32)).astype(jnp.bfloat16)
    return high, middle, low


def split_2(value):
    high = value.astype(jnp.bfloat16)
    low = (value - high.astype(jnp.float32)).astype(jnp.bfloat16)
    return high, low


def routes(n_tx, n_ty):
    found = {}
    for t, (ax, ay) in enumerate(SIDES):
        for u, (bx, by) in enumerate(SIDES):
            offset = (ax - bx, ay - by)
            if offset != (0, 0) and abs(offset[0]) < n_tx and abs(offset[1]) < n_ty:
                found.setdefault(offset, []).append((t, u))
    return sorted(found.items())


def kernel(
    n_tx,
    n_ty,
    raster_hbm,
    kernels_hbm,
    kw_hbm,
    cw_hbm,
    need_hbm,
    slot_hbm,
    row_hbm,
    level_hbm,
    weight_hbm,
    ids_hbm,
    jac_hbm,
    epe_ref,
    step_ref,
    raster_v,
    kernels_v,
    jac_v,
    kw_ref,
    cw_ref,
    need_ref,
    slot_ref,
    row_ref,
    level_ref,
    weight_ref,
    ids_ref,
    ids_s,
    q_own,
    edge_x,
    edge_y,
    halo_x,
    halo_y,
    q_ext,
    need_pad,
    choose,
    vec,
    contrib,
    energy,
    w_cols,
    u_cols,
    w_pad,
    sent,
    arrived,
    part_sums,
    all_sums,
    local_sem,
    hx_send,
    hx_recv,
    hy_send,
    hy_recv,
    ex_send,
    ex_recv,
    sum_send,
    sum_recv,
):
    n_dev = n_tx * n_ty
    gx, gy = raster_hbm.shape[0], raster_hbm.shape[1]
    pt_blocks = ids_ref.shape[1]
    nnz = ids_ref.shape[0]
    stride = BS // nnz
    seg_blocks = step_ref.shape[1] // BS
    n_kern = kw_ref.shape[0]
    span_y = gy + 2
    need = need_ref.shape[1]
    tx, ty = lax.axis_index("tx"), lax.axis_index("ty")
    rank = tx * n_ty + ty

    copy_k = pltpu.make_async_copy(kernels_hbm, kernels_v, local_sem.at[0])
    copy_r = pltpu.make_async_copy(raster_hbm, raster_v, local_sem.at[1])
    copy_j = pltpu.make_async_copy(jac_hbm, jac_v, local_sem.at[2])
    small = [
        pltpu.make_async_copy(source, target, local_sem.at[3 + i])
        for i, (source, target) in enumerate(
            (
                (kw_hbm, kw_ref),
                (cw_hbm, cw_ref),
                (need_hbm, need_ref),
                (slot_hbm, slot_ref),
                (row_hbm, row_ref),
                (level_hbm, level_ref),
                (weight_hbm, weight_ref),
                (ids_hbm, ids_ref),
                (ids_hbm, ids_s),
            )
        )
    ]
    small[0].start()
    small[1].start()
    copy_k.start()
    copy_r.start()
    for copy in small[2:]:
        copy.start()
    copy_j.start()

    def present(dx, dy):
        ok = None
        for pos, delta, count in ((tx, dx, n_tx), (ty, dy, n_ty)):
            test = None
            if delta < 0:
                test = pos + delta >= 0
            elif delta > 0:
                test = pos + delta < count
            if test is not None:
                ok = test if ok is None else jnp.logical_and(ok, test)
        return ok

    halo_x[...] = jnp.zeros_like(halo_x)
    halo_y[...] = jnp.zeros_like(halo_y)
    arrived[...] = jnp.zeros_like(arrived)
    ways = routes(n_tx, n_ty)

    barrier = pltpu.get_barrier_semaphore()

    def other(offset):
        peer = lax.rem(rank + offset, n_dev)
        return peer, {"tx": peer // n_ty, "ty": lax.rem(peer, n_ty)}

    @pl.loop(1, n_dev)
    def _(offset):
        pl.semaphore_signal(barrier, inc=1, device_id=other(offset)[1], device_id_type=MESH)

    small[0].wait()
    small[1].wait()
    copy_k.wait()
    cut = cw_ref[...]
    both = jnp.zeros((2 * BS, BS), jnp.float32)
    width = 4 * BS
    for chunk in range(2 * n_kern * BS // width):
        piece = kernels_v[:, chunk * width : (chunk + 1) * width]
        factor = jnp.concatenate(
            [cut * kw_ref[(chunk * 4 + i) // 2] for i in range(4)], axis=1
        )
        high, low = split_2(piece.astype(jnp.float32) * factor)
        both = both + lax.dot_general(
            jnp.concatenate([high, low], axis=0),
            piece,
            (((1,), (1,)), ((), ())),
            preferred_element_type=jnp.float32,
        )
    form = jnp.concatenate(split_2(both[:BS] + both[BS:]), axis=1)

    copy_r.wait()
    eye = lax.broadcasted_iota(jnp.int32, (1, BS, BS), 1) == lax.broadcasted_iota(
        jnp.int32, (1, BS, BS), 2
    )

    @pl.loop(0, gx, unroll=4)
    def _(a):
        rows = raster_v[a].reshape(gy * BS, BS)
        product = jnp.dot(rows, form, preferred_element_type=jnp.float32)
        terms = (product[:, :BS] + product[:, BS:]) * rows.astype(jnp.float32)
        column = jnp.sum(terms.reshape(gy, BS, BS), axis=2, keepdims=True)
        q = jnp.sum(jnp.where(eye, column, 0.0), axis=1)
        q_own[a] = q
        edge_y[0, pl.ds(a, 1), :] = q[0:1]
        edge_y[1, pl.ds(a, 1), :] = q[gy - 1 : gy]

    edge_x[0] = q_own[0]
    edge_x[1] = q_own[gx - 1]

    pl.semaphore_wait(barrier, n_dev - 1)

    halo_copies = []
    for side, dx in ((0, -1), (1, 1)):
        for dy in (-1, 0, 1):
            halo_copies.append(
                (
                    (dx, dy),
                    pltpu.make_async_remote_copy(
                        src_ref=edge_x.at[side],
                        dst_ref=halo_x.at[1 - side, 1 - dy],
                        send_sem=hx_send.at[side, 1 + dy],
                        recv_sem=hx_recv.at[1 - side, 1 - dy],
                        device_id={"tx": tx + dx, "ty": ty + dy},
                        device_id_type=MESH,
                    ),
                )
            )
    for side, dy in ((0, -1), (1, 1)):
        halo_copies.append(
            (
                (0, dy),
                pltpu.make_async_remote_copy(
                    src_ref=edge_y.at[side],
                    dst_ref=halo_y.at[1 - side],
                    send_sem=hy_send.at[side],
                    recv_sem=hy_recv.at[1 - side],
                    device_id={"tx": tx, "ty": ty + dy},
                    device_id_type=MESH,
                ),
            )
        )
    for (dx, dy), copy in halo_copies:

        @pl.when(present(dx, dy))
        def _():
            copy.start()

    q_ext[...] = jnp.zeros_like(q_ext)
    for a in range(gx):
        start = (a + 1) * span_y + 1
        q_ext[start : start + gy, :] = q_own[a]
    for copy in small[2:]:
        copy.wait()
    need_pad[...] = jnp.full(need_pad.shape, -1, jnp.int32)
    need_pad[:, :need] = need_ref[...]
    listed = (lax.broadcasted_iota(jnp.int32, (BS, BS), 0) == need_pad[...]).astype(jnp.float32).astype(
        jnp.bfloat16
    )
    choose[...] = jnp.zeros_like(choose)
    for k in range(nnz):
        choose[:, k * stride : k * stride + pt_blocks] = (
            lax.broadcasted_iota(jnp.int32, (choose.shape[0], pt_blocks), 0) == ids_ref[k : k + 1, :]
        ).astype(jnp.float32)
    pick_t = choose[...].astype(jnp.bfloat16)
    pick_t = jnp.concatenate([pick_t] * 3, axis=1)
    contrib[...] = jnp.zeros_like(contrib)
    vec[...] = jnp.zeros_like(vec)
    w_pad[...] = jnp.zeros_like(w_pad)
    for n in range(pt_blocks):
        w_pad[n : n + 1, :] = weight_ref[:, n * BS : (n + 1) * BS]
    turned = w_pad[...].T
    for n in range(pt_blocks):
        w_cols[n] = jnp.broadcast_to(turned[:, n : n + 1], (BS, BS))

    for side, dx in ((0, -1), (1, 1)):
        for dy in (-1, 0, 1):

            @pl.when(present(dx, dy))
            def _():
                pltpu.make_async_remote_copy(
                    src_ref=edge_x.at[side],
                    dst_ref=halo_x.at[side, 1 + dy],
                    send_sem=hx_send.at[side, 1 + dy],
                    recv_sem=hx_recv.at[side, 1 + dy],
                    device_id={"tx": tx + dx, "ty": ty + dy},
                    device_id_type=MESH,
                ).wait_recv()

    for side, dy in ((0, -1), (1, 1)):

        @pl.when(present(0, dy))
        def _():
            pltpu.make_async_remote_copy(
                src_ref=edge_y.at[side],
                dst_ref=halo_y.at[side],
                send_sem=hy_send.at[side],
                recv_sem=hy_recv.at[side],
                device_id={"tx": tx, "ty": ty + dy},
                device_id_type=MESH,
            ).wait_recv()

    for side in (0, 1):
        base = 0 if side == 0 else (gx + 1) * span_y
        q_ext[base + 1 : base + 1 + gy, :] = halo_x[side, 1]
        q_ext[base : base + 1, :] = halo_x[side, 0, gy - 1 : gy, :]
        q_ext[base + gy + 1 : base + gy + 2, :] = halo_x[side, 2, 0:1, :]
        for a in range(gx):
            at = (a + 1) * span_y + (0 if side == 0 else gy + 1)
            q_ext[at : at + 1, :] = halo_y[side, a : a + 1, :]

    table = jnp.concatenate(split_2(q_ext[...].T), axis=0)
    table = jnp.dot(table, listed, preferred_element_type=jnp.float32).astype(jnp.bfloat16)
    group = 2 * BS
    position = lax.broadcasted_iota(jnp.int32, (BS, group), 0)
    for piece in range(pt_blocks * BS // group):
        part = slice(piece * group, (piece + 1) * group)
        entry = (position == slot_ref[:, part]).astype(jnp.float32).astype(jnp.bfloat16)
        found = jnp.dot(table, entry, preferred_element_type=jnp.float32)
        found = found[:BS] + found[BS:]
        value = jnp.sum(
            jnp.where(position == row_ref[:, part], found, 0.0), axis=0, keepdims=True
        )
        error = value - level_ref[:, part]
        epe_ref[:, part] = error
        pulled = error * weight_ref[:, part]
        for i in range(group // BS):
            n = piece * (group // BS) + i
            w_pad[n : n + 1, :] = pulled[:, i * BS : (i + 1) * BS]
    turned = w_pad[...].T
    for n in range(pt_blocks):
        u_cols[n] = jnp.broadcast_to(turned[:, n : n + 1], (BS, BS))

    copy_j.wait()

    def way_copy(turn, way, flip):
        dx, dy = ways[way][0]
        sign = -1 if flip else 1
        return pltpu.make_async_remote_copy(
            src_ref=sent.at[turn, way],
            dst_ref=arrived.at[turn, way],
            send_sem=ex_send.at[turn, way],
            recv_sem=ex_recv.at[turn, way],
            device_id={"tx": tx + sign * dx, "ty": ty + sign * dy},
            device_id_type=MESH,
        )

    def start_terms(turn):
        summed = jnp.dot(
            pick_t,
            jnp.concatenate(split_3(contrib[...]), axis=0),
            preferred_element_type=jnp.float32,
        )
        parts = [summed[t * seg_blocks : (t + 1) * seg_blocks] for t in range(5)]
        for way, (offset, pairs) in enumerate(ways):
            for i, (t, u) in enumerate(pairs):
                sent[turn, way, i * seg_blocks : (i + 1) * seg_blocks, :] = parts[t]

            @pl.when(present(*offset))
            def _():
                way_copy(turn, way, False).start()

        return parts

    def end_terms(turn, parts):
        for way, ((dx, dy), pairs) in enumerate(ways):

            @pl.when(present(-dx, -dy))
            def _():
                way_copy(turn, way, True).wait_recv()

        total = list(parts)
        for way, (offset, pairs) in enumerate(ways):
            for i, (t, u) in enumerate(pairs):
                total[u] = total[u] + arrived[turn, way, i * seg_blocks : (i + 1) * seg_blocks, :]
        for u in range(1, 5):
            total[u] = jnp.where(present(*SIDES[u]), total[u], 0.0)
        return total

    def segments(u):
        return slice(u * seg_blocks, (u + 1) * seg_blocks)

    def forward(values):
        for u in range(5):
            vec[segments(u), :] = values[u]
        energy[...] = jnp.zeros_like(energy)

        @pl.loop(0, pt_blocks, unroll=UNROLL)
        def _(n):
            total = jac_v[n, 0] * vec[pl.ds(ids_s[0, n], 1), :]
            for k in range(1, nnz):
                total = total + jac_v[n, k] * vec[pl.ds(ids_s[k, n], 1), :]
            error = jnp.sum(total, axis=1, keepdims=True)
            scaled = error * w_cols[n]
            u_cols[n] = scaled
            energy[...] += jnp.sum((scaled * error).reshape(BS // 8, 8, BS), axis=0)

    def backward():
        @pl.loop(0, pt_blocks, unroll=UNROLL)
        def _(n):
            for k in range(nnz):
                contrib[pl.ds(k * stride + n, 1), :] = jnp.sum(
                    jac_v[n, k] * u_cols[n], axis=0, keepdims=True
                )

    def sum_copy(turn, offset, slot):
        peer, where = other(offset)
        at = rank if slot is None else peer
        return pltpu.make_async_remote_copy(
            src_ref=part_sums.at[turn],
            dst_ref=all_sums.at[turn, at],
            send_sem=sum_send.at[turn, offset],
            recv_sem=sum_recv.at[turn, at],
            device_id=where,
            device_id_type=MESH,
        )

    def start_sums(turn, own):
        square = jnp.sum(own * own, axis=0, keepdims=True)
        cross = jnp.sum(energy[...], axis=0, keepdims=True) * (1.0 / BS) + DAMPING * square
        both = jnp.concatenate([square, cross], axis=0)
        part_sums[turn] = both
        all_sums[turn, rank] = both

        @pl.loop(1, n_dev, unroll=5)
        def _(offset):
            sum_copy(turn, offset, None).start()

    def end_sums(turn):
        @pl.loop(1, n_dev, unroll=5)
        def _(offset):
            sum_copy(turn, offset, "theirs").wait_recv()

        total = jnp.sum(jnp.sum(all_sums[turn], axis=0), axis=1, keepdims=True)
        return total[0:1], total[1:2]

    backward()
    residual = [-part for part in end_terms(0, start_terms(0))]
    direction = along = step = norm_now = alpha = None
    for turn in range(SUMS):
        last = turn + 1 == SUMS
        forward(residual)
        start_sums(turn, residual[0])
        if not last:
            backward()
            parts = start_terms(turn + 1)
        if last:
            for (dx, dy), copy in halo_copies:

                @pl.when(present(dx, dy))
                def _():
                    copy.wait_send()

            for before in range(TURNS):
                for way, (offset, pairs) in enumerate(ways):

                    @pl.when(present(*offset))
                    def _():
                        way_copy(before, way, False).wait_send()

            for before in range(SUMS):

                @pl.loop(1, n_dev, unroll=5)
                def _(offset):
                    sum_copy(before, offset, None).wait_send()

        else:
            image = [
                part + DAMPING * value
                for part, value in zip(end_terms(turn + 1, parts), residual)
            ]
        norm_next, product = end_sums(turn)
        if turn == 0:
            alpha = norm_next / product
            direction, step = residual[0], alpha * residual[0]
            along = image
        else:
            ratio = norm_next / norm_now
            alpha = norm_next / (product - ratio * norm_next / alpha)
            direction = residual[0] + ratio * direction
            step = step + alpha * direction
            if not last:
                along = [new + ratio * old for new, old in zip(image, along)]
        norm_now = norm_next
        if not last:
            residual = [value - alpha * change for value, change in zip(residual, along)]

    for j in range(seg_blocks):
        step_ref[:, j * BS : (j + 1) * BS] = step[j : j + 1, :]


def deliver(epe_v, step_v, epe_hbm, step_hbm, sem):
    copies = [
        pltpu.make_async_copy(epe_v, epe_hbm, sem.at[0]),
        pltpu.make_async_copy(step_v, step_hbm, sem.at[1]),
    ]
    for copy in copies:
        copy.start()
    for copy in copies:
        copy.wait()


def on_device(
    n_tx,
    n_ty,
    raster,
    kernels,
    kernel_weights,
    cut_weights,
    need_list,
    point_slot,
    point_row,
    threshold,
    point_weight,
    jac_ids,
    jacobian,
):
    points = point_slot.shape[-1]
    pt_blocks, nnz = jac_ids.shape[-2:]
    gx, gy = raster.shape[:2]
    segments = SEG
    wide = 2 * (SEG // BS)
    n_ways = len(routes(n_tx, n_ty))
    n_dev = n_tx * n_ty
    f32 = jnp.float32
    vmem = pl.BlockSpec(memory_space=pltpu.VMEM)
    anywhere = pl.BlockSpec(memory_space=pl.ANY)
    dma = pltpu.SemaphoreType.DMA
    epe, step = pl.pallas_call(
        functools.partial(kernel, n_tx, n_ty),
        out_shape=(
            jax.ShapeDtypeStruct((1, points), f32),
            jax.ShapeDtypeStruct((1, segments), f32),
        ),
        in_specs=[anywhere] * 11,
        out_specs=(vmem, vmem),
        scratch_shapes=[
            pltpu.VMEM(raster.shape, jnp.bfloat16),
            pltpu.VMEM(kernels.shape, jnp.bfloat16),
            pltpu.VMEM((pt_blocks, nnz, BS, BS), f32),
            pltpu.SMEM(kernel_weights.shape, f32),
            pltpu.VMEM((1, BS), f32),
            pltpu.VMEM((1, need_list.shape[-1]), jnp.int32),
            pltpu.VMEM((1, points), jnp.int32),
            pltpu.VMEM((1, points), jnp.int32),
            pltpu.VMEM((1, points), f32),
            pltpu.VMEM((1, points), f32),
            pltpu.VMEM((nnz, pt_blocks), jnp.int32),
            pltpu.SMEM((nnz, pt_blocks), jnp.int32),
            pltpu.VMEM((gx, gy, BS), f32),
            pltpu.VMEM((2, gy, BS), f32),
            pltpu.VMEM((2, gx, BS), f32),
            pltpu.VMEM((2, 3, gy, BS), f32),
            pltpu.VMEM((2, gx, BS), f32),
            pltpu.VMEM((BS, BS), f32),
            pltpu.VMEM((1, BS), jnp.int32),
            pltpu.VMEM((64, BS), f32),
            pltpu.VMEM((64, BS), f32),
            pltpu.VMEM((BS, BS), f32),
            pltpu.VMEM((8, BS), f32),
            pltpu.VMEM((pt_blocks, BS, BS), f32),
            pltpu.VMEM((pt_blocks, BS, BS), f32),
            pltpu.VMEM((BS, BS), f32),
            pltpu.VMEM((TURNS, n_ways, wide, BS), f32),
            pltpu.VMEM((TURNS, n_ways, wide, BS), f32),
            pltpu.VMEM((SUMS, 2, BS), f32),
            pltpu.VMEM((SUMS, n_dev, 2, BS), f32),
            dma((12,)),
            dma((2, 3)),
            dma((2, 3)),
            dma((2,)),
            dma((2,)),
            dma((TURNS, n_ways)),
            dma((TURNS, n_ways)),
            dma((SUMS, n_dev)),
            dma((SUMS, n_dev)),
        ],
        compiler_params=pltpu.CompilerParams(
            collective_id=0, has_side_effects=True, vmem_limit_bytes=56 * 1024 * 1024
        ),
    )(
        raster,
        kernels,
        kernel_weights,
        cut_weights.reshape(1, BS),
        need_list.reshape(1, -1),
        point_slot.reshape(1, points),
        point_row.reshape(1, points),
        threshold.reshape(1, points),
        point_weight.reshape(1, points),
        jac_ids.reshape(pt_blocks, nnz).T,
        jacobian.reshape(pt_blocks, nnz, BS, BS),
    )
    epe, step = pl.pallas_call(
        deliver,
        out_shape=(
            jax.ShapeDtypeStruct((1, points), f32),
            jax.ShapeDtypeStruct((1, segments), f32),
        ),
        in_specs=[vmem, vmem],
        out_specs=(anywhere, anywhere),
        scratch_shapes=[dma((2,))],
    )(epe, step)
    return epe.reshape(1, 1, points), step.reshape(1, 1, segments)


def solution(mesh):
    tiles = ("grp", "tx")
    in_specs = (
        P(tiles, "ty", None, None),
        P(),
        P(),
        P(),
        P(tiles, "ty", None),
        P(tiles, "ty", None),
        P(tiles, "ty", None),
        P(tiles, "ty", None),
        P(tiles, "ty", None),
        P(tiles, "ty", None, None),
        P(tiles, "ty", None, None, None, None),
    )
    out_specs = (P(tiles, "ty", None), P(tiles, "ty", None))
    return jax.shard_map(
        functools.partial(on_device, mesh.shape["tx"], mesh.shape["ty"]),
        mesh=mesh,
        in_specs=in_specs,
        out_specs=out_specs,
        check_vma=False,
    )
```
